128 devices in a mesh: feat: 64 (over y, x, z), batch: 2 (over core).
Axes of the slice: x: 4, y: 4, z: 4, core: 2. Of those that a mesh axis runs over, the one named last changes fastest.
Arguments:
- features: bfloat16 [1024, 131072], P('batch', 'feat'), may hold values from -6 to 6
- cotangent: bfloat16 [1024, 131072], P('batch', 'feat'), may hold values from -6 to 6
- u_rows: bfloat16 [131072, 1024], P('feat'), may hold values from -0.1875 to 0.1875
- v_rows: bfloat16 [131072, 1024], P('feat'), may hold values from -0.046875 to 0.046875
- bias: float32 [131072], P('feat'), may hold values from -6 to 6
Outputs:
- grad_input: bfloat16 [1024, 131072], P('batch', 'feat')
- grad_u: bfloat16 [131072, 1024], P('feat', 'batch')
- grad_v: bfloat16 [131072, 1024], P('feat', 'batch')
- grad_bias: float32 [131072], P('feat')
The draws below stay inside these ranges and needn't reach their ends.
All inputs are finite; a program needn't handle non-finite values.
Results may differ from the reference program's by a relative error of at most 0.0065.
Values may be sent and summed in bfloat16 or wider, within the bound.
A program may use at most 128 MiB of HBM per device.

```python
import jax
import jax.numpy as jnp
from jax import lax

RANK = 1024
WIDTH = 131072
SAMPLES = 1024


def raised(result, own_key, source, target, blocks, factor):
    owner, partner = [(jnp.arange(result.shape[dim]) // (result.shape[dim] // blocks)).reshape([-1 if axis == dim else 1 for axis in range(result.ndim)]) for dim in (source, target)]
    chosen = jax.random.permutation(own_key, blocks)[partner]
    strong = (owner == chosen) | (owner == (partner + blocks // 2) % blocks)
    return jnp.where(strong, factor * result, result)


def steps_of(stream_key, dims, cuts, least, largest):
    level, own = 1.0, jax.random.fold_in(stream_key, 6)
    for dim, parts in cuts:
        steps = jnp.exp(jax.random.uniform(jax.random.fold_in(own, dim), (parts,), jnp.float32, least / len(cuts), largest / len(cuts)))
        level = level * jnp.repeat(steps, dims[dim] // parts).reshape([-1 if axis == dim else 1 for axis in range(len(dims))])
    return level


def gaussian(own_key, extent, spread, bound, pieces=(), held_as=jnp.bfloat16):
    loudness = steps_of(own_key, extent, pieces, -0.22, 0.18) if pieces else 1.0
    result = jax.random.normal(own_key, extent, jnp.float32) * spread * loudness
    return jnp.minimum(jnp.maximum(result, -bound), bound).astype(held_as)


def gaussian_with(key, dims, width, limit, split, heavy, kind=jnp.bfloat16):
    values = width * jax.random.normal(key, dims, jnp.float32)
    if split:
        values = values * steps_of(key, dims, split, -0.22, 0.18)
    return jnp.clip(raised(values, jax.random.fold_in(key, 3), *heavy), -limit, limit).astype(kind)


def setup_inputs(seed: int = 0) -> dict:
    splits = jax.random.split(jax.random.key(seed), 6)
    features = gaussian(splits[0], (SAMPLES, WIDTH), 1.0, 6.0, ((0, 2), (1, 64)))
    cotangent = gaussian(splits[1], (SAMPLES, WIDTH), 1.0, 6.0, ((0, 2), (1, 64)))
    u_rows = gaussian(splits[2], (WIDTH, RANK), RANK ** -0.5, 0.1875, ((0, 64),))
    v_rows = gaussian_with(splits[3], (WIDTH, RANK), WIDTH ** -0.5, 0.046875, ((0, 64),), (0, 1, 64, 4.0))
    bias = gaussian(splits[4], (WIDTH,), 1.0, 6.0, ((0, 64),), jnp.float32)
    return {"features": features, "cotangent": cotangent, "u_rows": u_rows, "v_rows": v_rows, "bias": bias}


def reference(features, cotangent, u_rows, v_rows, bias):
    codes = jnp.dot(features, v_rows, preferred_element_type=jnp.float32).astype(jnp.bfloat16)
    lifted = lax.dot_general(codes, u_rows, (((1,), (1,)), ((), ())), preferred_element_type=jnp.float32)
    grad_out = cotangent.astype(jnp.float32)
    dlift = (grad_out * features.astype(jnp.float32)).astype(jnp.bfloat16)
    dcodes = jnp.dot(dlift, u_rows, preferred_element_type=jnp.float32).astype(jnp.bfloat16)
    back = lax.dot_general(dcodes, v_rows, (((1,), (1,)), ((), ())), preferred_element_type=jnp.float32)
    grad_input = (grad_out * (lifted + bias[None, :] + 1.0) + back).astype(jnp.bfloat16)
    grad_u = lax.dot_general(dlift, codes, (((0,), (0,)), ((), ())), preferred_element_type=jnp.float32).astype(jnp.bfloat16)
    grad_v = lax.dot_general(features, dcodes, (((0,), (0,)), ((), ())), preferred_element_type=jnp.float32).astype(jnp.bfloat16)
    grad_bias = jnp.sum(dlift.astype(jnp.float32), axis=0)
    return grad_input, grad_u, grad_v, grad_bias
```

```python
import jax
import jax.numpy as jnp
from jax import lax
from jax.experimental import pallas as pl
from jax.experimental.pallas import tpu as pltpu
from jax.sharding import PartitionSpec as P

MESH = pl.DeviceIdType.MESH
F32, BF16 = jnp.float32, jnp.bfloat16
ROWS, COLS, RANK = 512, 2048, 1024
BLOCK = 256
TILES = 256
HALVINGS, DIMS = 4, 6
STAGES = DIMS + HALVINGS
SIZES = ((48, 48, 48, 48, 32, 32), (48, 48, 48, 32, 32, 48))
TURNS = (0, 3)
AXES = ((16, 0), (4, 0), (1, 0), (16, 1), (4, 1), (1, 1))


def partners(feat):
    bits, others = [], []
    for stride, kind in AXES:
        place = lax.rem(lax.div(feat, stride), 4)
        if kind == 0:
            bits.append(lax.rem(lax.div(place + 1, 2), 2))
            other = place + 1 - 2 * lax.rem(place, 2)
        else:
            bits.append(lax.div(place, 2))
            other = 3 - place
        others.append(feat + (other - place) * stride)
    return bits, others


class Sum:
    def __init__(self, index, bits, others, core, acc, out, got, mid, full, send_sem, recv_sem):
        self.index, self.bits, self.others, self.core = index, bits, others, core
        self.acc, self.out, self.got, self.mid, self.full = acc, out, got, mid, full
        self.send_sem, self.recv_sem = send_sem, recv_sem
        self.sizes = SIZES[index]
        self.starts = [sum(self.sizes[:part]) for part in range(6)]
        self.copies, self.region, self.past = {}, {}, {}
        offset, self.offset = 0, {}
        for stage in range(DIMS):
            for part in range(6):
                self.offset[stage, part] = offset
                offset += self.sizes[part] >> min(stage + 1, HALVINGS)
        offset, self.place = 0, {}
        for stage in range(HALVINGS, DIMS):
            for part in range(6):
                self.place[stage, part] = offset
                offset += self.sizes[part] >> HALVINGS

    def dim(self, part, stage):
        return (part + stage + TURNS[self.index]) % DIMS

    def start(self, part, stage, source, target):
        copy = pltpu.make_async_remote_copy(
            src_ref=source,
            dst_ref=target,
            send_sem=self.send_sem.at[stage, part],
            recv_sem=self.recv_sem.at[stage, part],
            device_id=(self.others[self.dim(part, stage if stage < DIMS else STAGES - 1 - stage)], self.core),
            device_id_type=MESH,
        )
        copy.start()
        self.copies[stage, part] = copy

    def send(self, part, stage):
        if stage == 0:
            self.region[part] = (self.starts[part], self.sizes[part])
        start, size = self.region[part]
        if stage < HALVINGS:
            half = size // 2
            bit = self.bits[self.dim(part, stage)]
            away = start + (1 - bit) * half
            self.past[part, stage] = start
            self.region[part] = (start + bit * half, half)
            self.start(part, stage, self.out.at[pl.ds(away, half)], self.got.at[pl.ds(self.offset[stage, part], half)])
        elif stage < DIMS:
            self.start(part, stage, self.mid.at[pl.ds(self.place[stage, part], size)], self.got.at[pl.ds(self.offset[stage, part], size)])
        else:
            where = self.full.at[pl.ds(start, size)]
            self.start(part, stage, where, where)

    def receive(self, part, stage):
        self.copies[stage, part].wait_recv()
        start, size = self.region[part]
        if stage < DIMS:
            here = pl.ds(start, size)
            value = self.acc[here] + self.got[pl.ds(self.offset[stage, part], size)].astype(F32)
            if stage == DIMS - 1:
                self.full[here] = value.astype(BF16)
            else:
                self.acc[here] = value
                if stage + 1 < HALVINGS:
                    self.out[here] = value.astype(BF16)
                else:
                    self.mid[pl.ds(self.place[stage + 1, part], size)] = value.astype(BF16)
        else:
            self.region[part] = (self.past[part, STAGES - 1 - stage], 2 * size)

    def step(self, stage):
        for part in range(6):
            self.receive(part, stage)
            if stage + 1 < STAGES:
                self.send(part, stage + 1)

    def finish(self):
        for copy in self.copies.values():
            copy.wait_send()


def kernel(
    f_hbm, c_hbm, u_hbm, v_hbm, b_ref, gi_hbm, gu_hbm, gv_hbm, gb_ref,
    f, c, u, v, d, acc_a, acc_b, out_a, out_b, got_a, got_b, mid_a, mid_b, full_a, full_b,
    ft, dt, base, codes, dcodes, half_a, half_b, twin_a, twin_b, gi, gu, gv, bias_own, bias_twin,
    load_sem, store_sem, send_a, recv_a, send_b, recv_b, twin_send, twin_recv,
):
    feat, core = lax.axis_index("feat"), lax.axis_index("batch")
    twin = (feat, 1 - core)
    bits, others = partners(feat)

    loads = [pltpu.make_async_copy(f_hbm, f, load_sem.at[0])]
    for j in range(4):
        cols = pl.ds(j * BLOCK, BLOCK)
        loads.append(pltpu.make_async_copy(v_hbm.at[:, cols], v.at[:, cols], load_sem.at[1 + j]))
    loads.append(pltpu.make_async_copy(c_hbm, c, load_sem.at[5]))
    for j in range(4):
        cols = pl.ds(j * BLOCK, BLOCK)
        loads.append(pltpu.make_async_copy(u_hbm.at[:, cols], u.at[:, cols], load_sem.at[6 + j]))
    for load in loads:
        load.start()

    barrier = pltpu.get_barrier_semaphore()
    for other in others:
        pl.semaphore_signal(barrier, inc=1, device_id=(other, core), device_id_type=MESH)
    pl.semaphore_signal(barrier, inc=1, device_id=twin, device_id_type=MESH)

    sum_a = Sum(0, bits, others, core, acc_a, out_a, got_a, mid_a, full_a, send_a, recv_a)
    sum_b = Sum(1, bits, others, core, acc_b, out_b, got_b, mid_b, full_b, send_b, recv_b)

    def partial(left, right, total, j):
        block = jnp.dot(left[...], right[:, j * BLOCK:(j + 1) * BLOCK], preferred_element_type=F32)
        for side in range(2):
            tiles = block[:, side * 128:(side + 1) * 128].reshape(32, 16, 128)
            where = pl.ds(64 * j + 32 * side, 32)
            total.acc[where] = tiles
            total.out[where] = tiles.astype(BF16)

    def first_sends(total, j):
        for part in range(6):
            end = total.starts[part] + total.sizes[part]
            if 64 * j < end <= 64 * (j + 1):
                total.send(part, 0)

    loads[0].wait()
    for j in range(4):
        loads[1 + j].wait()
        partial(f, v, sum_a, j)
        if j == 0:
            pl.semaphore_wait(barrier, 7)
        first_sends(sum_a, j)

    loads[5].wait()

    @pl.loop(0, COLS // BLOCK)
    def _(i):
        cols = pl.ds(pl.multiple_of(i * BLOCK, BLOCK), BLOCK)
        lift = (c[:, cols].astype(F32) * f[:, cols].astype(F32)).astype(BF16)
        d[:, cols] = lift
        bias_own[:, cols] = jnp.broadcast_to(jnp.sum(lift.astype(F32), axis=0, keepdims=True), (8, BLOCK))

    for j in range(4):
        loads[6 + j].wait()
        partial(d, u, sum_b, j)
        first_sends(sum_b, j)

    def to_twin(source, target, k):
        copy = pltpu.make_async_remote_copy(
            src_ref=source, dst_ref=target, send_sem=twin_send.at[k], recv_sem=twin_recv.at[k],
            device_id=twin, device_id_type=MESH,
        )
        copy.start()
        return copy

    to_twins = [to_twin(bias_own, bias_twin, 0)]
    for k, (source, target) in enumerate(((d, dt), (f, ft))):
        @pl.loop(0, COLS // 128)
        def _(i):
            at = pl.multiple_of(i * 128, 128)
            target[core, pl.ds(at, 128), :] = source[:, pl.ds(at, 128)].T

        to_twins.append(to_twin(target.at[core], target.at[core], 1 + k))

    for stage in range(STAGES):
        sum_a.step(stage)
        sum_b.step(stage)

    to_twins.append(to_twin(full_a.at[pl.ds((1 - core) * 128, 128)], twin_a, 3))
    to_twins.append(to_twin(full_b.at[pl.ds((1 - core) * 128, 128)], twin_b, 4))

    for full, flat, half in ((full_a, codes, half_a), (full_b, dcodes, half_b)):
        for j in range(8):
            flat[:, j * 128:(j + 1) * 128] = full[32 * j:32 * (j + 1)].reshape(ROWS, 128)
        for j in range(4):
            half[core, :, j * 128:(j + 1) * 128] = full[pl.ds(core * 128 + 32 * j, 32)].reshape(ROWS, 128)

    nt = (((1,), (1,)), ((), ()))

    @pl.loop(0, COLS // BLOCK)
    def _(i):
        cols = pl.ds(pl.multiple_of(i * BLOCK, BLOCK), BLOCK)
        lifted = lax.dot_general(codes[...], u[cols, :], nt, preferred_element_type=F32)
        base[:, cols] = c[:, cols].astype(F32) * (lifted + b_ref[:, cols] + 1.0)

    @pl.loop(0, COLS // BLOCK)
    def _(i):
        cols = pl.ds(pl.multiple_of(i * BLOCK, BLOCK), BLOCK)
        back = lax.dot_general(dcodes[...], v[cols, :], nt, preferred_element_type=F32)
        gi[:, cols] = (base[:, cols] + back).astype(BF16)
        pltpu.make_async_copy(gi.at[:, cols], gi_hbm.at[:, cols], store_sem.at[0, i]).start()

    for k, (other, half) in enumerate(((twin_a, half_a), (twin_b, half_b))):
        to_twins[3 + k].wait_recv()
        for j in range(4):
            half[1 - core, :, j * 128:(j + 1) * 128] = other[32 * j:32 * (j + 1)].reshape(ROWS, 128)

    for k, (left, right, result, target) in enumerate(((dt, half_a, gu, gu_hbm), (ft, half_b, gv, gv_hbm))):
        to_twins[1 + k].wait_recv()

        @pl.loop(0, COLS // BLOCK)
        def _(i):
            rows = pl.ds(pl.multiple_of(i * BLOCK, BLOCK), BLOCK)
            value = jnp.dot(left[0, rows, :], right[0], preferred_element_type=F32)
            value += jnp.dot(left[1, rows, :], right[1], preferred_element_type=F32)
            result[rows, :] = value.astype(BF16)
            pltpu.make_async_copy(result.at[rows, :], target.at[rows, :], store_sem.at[1 + k, i]).start()

    to_twins[0].wait_recv()
    gb_ref[...] = bias_own[0:1, :] + bias_twin[0:1, :]

    @pl.loop(0, COLS // BLOCK)
    def _(i):
        cols = pl.ds(pl.multiple_of(i * BLOCK, BLOCK), BLOCK)
        pltpu.make_async_copy(gi.at[:, cols], gi_hbm.at[:, cols], store_sem.at[0, i]).wait()
        pltpu.make_async_copy(gu.at[cols, :], gu_hbm.at[cols, :], store_sem.at[1, i]).wait()
        pltpu.make_async_copy(gv.at[cols, :], gv_hbm.at[cols, :], store_sem.at[2, i]).wait()

    sum_a.finish()
    sum_b.finish()
    for copy in to_twins:
        copy.wait_send()


def shards(features, cotangent, u_rows, v_rows, bias):
    anywhere, vmem = pl.BlockSpec(memory_space=pl.ANY), pl.BlockSpec(memory_space=pltpu.VMEM)
    tiles = (TILES, 16, 128)
    dma = pltpu.SemaphoreType.DMA
    grad_input, grad_u, grad_v, grad_bias = pl.pallas_call(
        kernel,
        out_shape=(
            jax.ShapeDtypeStruct((ROWS, COLS), BF16),
            jax.ShapeDtypeStruct((COLS, RANK // 2), BF16),
            jax.ShapeDtypeStruct((COLS, RANK // 2), BF16),
            jax.ShapeDtypeStruct((1, COLS), F32),
        ),
        in_specs=[anywhere] * 4 + [vmem],
        out_specs=(anywhere, anywhere, anywhere, vmem),
        scratch_shapes=[
            pltpu.VMEM((ROWS, COLS), BF16), pltpu.VMEM((ROWS, COLS), BF16),
            pltpu.VMEM((COLS, RANK), BF16), pltpu.VMEM((COLS, RANK), BF16),
            pltpu.VMEM((ROWS, COLS), BF16),
            pltpu.VMEM(tiles, F32), pltpu.VMEM(tiles, F32),
            pltpu.VMEM(tiles, BF16), pltpu.VMEM(tiles, BF16),
            pltpu.VMEM((272, 16, 128), BF16), pltpu.VMEM((272, 16, 128), BF16),
            pltpu.VMEM((32, 16, 128), BF16), pltpu.VMEM((32, 16, 128), BF16),
            pltpu.VMEM(tiles, BF16), pltpu.VMEM(tiles, BF16),
            pltpu.VMEM((2, COLS, ROWS), BF16), pltpu.VMEM((2, COLS, ROWS), BF16),
            pltpu.VMEM((ROWS, COLS), F32),
            pltpu.VMEM((ROWS, RANK), BF16), pltpu.VMEM((ROWS, RANK), BF16),
            pltpu.VMEM((2, ROWS, RANK // 2), BF16), pltpu.VMEM((2, ROWS, RANK // 2), BF16),
            pltpu.VMEM((128, 16, 128), BF16), pltpu.VMEM((128, 16, 128), BF16),
            pltpu.VMEM((ROWS, COLS), BF16),
            pltpu.VMEM((COLS, RANK // 2), BF16), pltpu.VMEM((COLS, RANK // 2), BF16),
            pltpu.VMEM((8, COLS), F32), pltpu.VMEM((8, COLS), F32),
            dma((10,)), dma((3, COLS // BLOCK)),
            dma((STAGES, 6)), dma((STAGES, 6)), dma((STAGES, 6)), dma((STAGES, 6)),
            dma((5,)), dma((5,)),
        ],
        compiler_params=pltpu.CompilerParams(collective_id=0, has_side_effects=True, vmem_limit_bytes=60 << 20),
    )(features, cotangent, u_rows, v_rows, bias.reshape(1, COLS))
    return grad_input, grad_u, grad_v, grad_bias.reshape(COLS)


def solution(mesh):
    in_specs = (P("batch", "feat"), P("batch", "feat"), P("feat", None), P("feat", None), P("feat"))
    out_specs = (P("batch", "feat"), P("feat", "batch"), P("feat", "batch"), P("feat"))
    return jax.shard_map(shards, mesh=mesh, in_specs=in_specs, out_specs=out_specs, check_vma=False)
```

```python
import jax
import jax.numpy as jnp
from jax import lax
from jax.experimental import pallas as pl
from jax.experimental.pallas import tpu as pltpu
from jax.sharding import PartitionSpec as P

MESH = pl.DeviceIdType.MESH
F32, BF16 = jnp.float32, jnp.bfloat16
NT = (((1,), (1,)), ((), ()))
ROWS, COLS, RANK = 512, 2048, 1024
HALF, BLOCK = RANK // 2, 256
BLOCKS = COLS // BLOCK
TILES = 256
STAGES, PARTS = 5, 3
SIZES = ((96, 80, 80), (80, 96, 80))
AXES = ((16, 0), (4, 0), (1, 0), (16, 1), (4, 1), (1, 1))
PAIRS = ((0, 4), (1, 5), (2, 3))


def hypercube(feat):
    bits, steps = [], []
    for stride, kind in AXES:
        place = lax.rem(lax.div(feat, stride), 4)
        if kind == 0:
            bits.append(lax.rem(lax.div(place + 1, 2), 2))
            steps.append((1 - 2 * lax.rem(place, 2)) * stride)
        else:
            bits.append(lax.div(place, 2))
            steps.append((3 - 2 * place) * stride)
    return bits, steps


def squares(feat):
    bits, steps = hypercube(feat)
    result = []
    for high, low in PAIRS:
        quarters, chips = [], []
        for flip in range(4):
            far, near = flip // 2, flip % 2
            quarters.append(2 * (1 - bits[high] if far else bits[high]) + (1 - bits[low] if near else bits[low]))
            chips.append(feat + far * steps[high] + near * steps[low])
        result.append((quarters, chips))
    return result


class Sum:
    def __init__(self, index, places, core, acc, out, got, mid, full, send_sem, recv_sem):
        self.index, self.places, self.core = index, places, core
        self.acc, self.out, self.got, self.mid, self.full = acc, out, got, mid, full
        self.send_sem, self.recv_sem = send_sem, recv_sem
        self.sizes = SIZES[index]
        self.starts = [sum(self.sizes[:part]) for part in range(PARTS)]
        self.copies, self.past = {}, {}
        self.region = dict(enumerate(zip(self.starts, self.sizes)))
        offset, self.offset = 0, {}
        for stage in range(3):
            for part in range(PARTS):
                self.offset[stage, part] = offset
                offset += 3 * (self.sizes[part] >> min(2 * stage + 2, 4))

    def square(self, part, stage):
        return self.places[(part + min(stage, STAGES - 1 - stage) + self.index) % PARTS]

    def slot(self, part, stage, flip, size):
        return pl.ds(self.offset[stage, part] + (flip - 1) * size, size)

    def send(self, part, stage):
        quarters, chips = self.square(part, stage)
        start, size = self.region[part]
        if stage < 2:
            size //= 4
            self.past[stage, part] = start
            self.region[part] = (start + quarters[0] * size, size)
        for flip in (3, 2, 1):
            if stage < 2:
                source = self.out.at[pl.ds(start + quarters[flip] * size, size)]
                target = self.got.at[self.slot(part, stage, flip, size)]
            elif stage == 2:
                source = self.mid.at[pl.ds(self.starts[part] // 16, size)]
                target = self.got.at[self.slot(part, stage, flip, size)]
            else:
                source = target = self.full.at[pl.ds(start, size)]
            copy = pltpu.make_async_remote_copy(
                src_ref=source,
                dst_ref=target,
                send_sem=self.send_sem.at[stage, part, flip - 1],
                recv_sem=self.recv_sem.at[stage, part, flip - 1],
                device_id=(chips[flip], self.core),
                device_id_type=MESH,
            )
            copy.start()
            self.copies[stage, part, flip] = copy

    def receive(self, part, stage):
        for flip in (1, 2, 3):
            self.copies[stage, part, flip].wait_recv()
        start, size = self.region[part]
        if stage > 2:
            self.region[part] = (self.past[STAGES - 1 - stage, part], 4 * size)
            return
        here = pl.ds(start, size)
        value = self.acc[here]
        for flip in (1, 2, 3):
            value += self.got[self.slot(part, stage, flip, size)].astype(F32)
        if stage == 2:
            self.full[here] = value.astype(BF16)
            return
        self.acc[here] = value
        if stage == 0:
            self.out[here] = value.astype(BF16)
        else:
            self.mid[pl.ds(self.starts[part] // 16, size)] = value.astype(BF16)

    def step(self, stage):
        for part in range(PARTS):
            self.receive(part, stage)
            if stage + 1 < STAGES:
                self.send(part, stage + 1)

    def finish(self):
        for copy in self.copies.values():
            copy.wait_send()


def kernel(
    f_hbm, c_hbm, u_hbm, v_hbm, b_ref, gi, gu, ft, half_b, gb_ref,
    f, c, u, v, d, acc_a, acc_b, out_a, out_b, got_a, got_b, mid_a, mid_b, full_a, full_b,
    dt, base, codes, dcodes, half_a, twin_a, twin_b, bias_own, bias_twin,
    load_sem, send_a, recv_a, send_b, recv_b, twin_send, twin_recv,
):
    feat, core = lax.axis_index("feat"), lax.axis_index("batch")
    twin = (feat, 1 - core)
    places = squares(feat)

    loads = [pltpu.make_async_copy(f_hbm, f, load_sem.at[0])]
    for j in range(4):
        cols = pl.ds(j * BLOCK, BLOCK)
        loads.append(pltpu.make_async_copy(v_hbm.at[:, cols], v.at[:, cols], load_sem.at[1 + j]))
    loads.append(pltpu.make_async_copy(c_hbm, c, load_sem.at[5]))
    for j in range(4):
        cols = pl.ds(j * BLOCK, BLOCK)
        loads.append(pltpu.make_async_copy(u_hbm.at[:, cols], u.at[:, cols], load_sem.at[6 + j]))
    for load in loads:
        load.start()

    barrier = pltpu.get_barrier_semaphore()
    for _, chips in places:
        for flip in (1, 2, 3):
            pl.semaphore_signal(barrier, inc=1, device_id=(chips[flip], core), device_id_type=MESH)
    pl.semaphore_signal(barrier, inc=1, device_id=twin, device_id_type=MESH)

    sum_a = Sum(0, places, core, acc_a, out_a, got_a, mid_a, full_a, send_a, recv_a)
    sum_b = Sum(1, places, core, acc_b, out_b, got_b, mid_b, full_b, send_b, recv_b)

    def partial(left, right, total, j):
        block = jnp.dot(left[...], right[:, j * BLOCK:(j + 1) * BLOCK], preferred_element_type=F32)
        for side in range(2):
            tiles = block[:, side * 128:(side + 1) * 128].reshape(32, 16, 128)
            where = pl.ds(64 * j + 32 * side, 32)
            total.acc[where] = tiles
            total.out[where] = tiles.astype(BF16)

    def first_sends(total, j):
        for part in range(PARTS):
            end = total.starts[part] + total.sizes[part]
            if 64 * j < end <= 64 * (j + 1):
                total.send(part, 0)

    loads[0].wait()
    for j in range(4):
        loads[1 + j].wait()
        partial(f, v, sum_a, j)
        if j == 1:
            pl.semaphore_wait(barrier, 10)
        first_sends(sum_a, j)

    loads[5].wait()

    @pl.loop(0, BLOCKS)
    def _(i):
        cols = pl.ds(pl.multiple_of(i * BLOCK, BLOCK), BLOCK)
        lift = (c[:, cols].astype(F32) * f[:, cols].astype(F32)).astype(BF16)
        d[:, cols] = lift
        bias_own[:, cols] = jnp.broadcast_to(jnp.sum(lift.astype(F32), axis=0, keepdims=True), (8, BLOCK))

    for j in range(4):
        loads[6 + j].wait()
        partial(d, u, sum_b, j)
        first_sends(sum_b, j)

    def to_twin(source, target, k):
        copy = pltpu.make_async_remote_copy(
            src_ref=source, dst_ref=target, send_sem=twin_send.at[k], recv_sem=twin_recv.at[k],
            device_id=twin, device_id_type=MESH,
        )
        copy.start()
        return copy

    to_twins = [to_twin(bias_own, bias_twin, 0)]
    for k, (source, target) in enumerate(((d, dt), (f, ft))):

        @pl.loop(0, COLS // 128)
        def _(i):
            at = pl.multiple_of(i * 128, 128)
            target[core, pl.ds(at, 128), :] = source[:, pl.ds(at, 128)].T

        to_twins.append(to_twin(target.at[core], target.at[core], 1 + k))

    def flatten(full, flat, half):
        for j in range(8):
            flat[:, j * 128:(j + 1) * 128] = full[32 * j:32 * (j + 1)].reshape(ROWS, 128)
        for j in range(4):
            half[core, :, j * 128:(j + 1) * 128] = full[pl.ds(core * 128 + 32 * j, 32)].reshape(ROWS, 128)

    def other_half(other, half):
        for j in range(4):
            half[1 - core, :, j * 128:(j + 1) * 128] = other[32 * j:32 * (j + 1)].reshape(ROWS, 128)

    sum_a.step(0)
    sum_a.step(1)
    sum_b.step(0)
    sum_a.step(2)
    sum_b.step(1)
    sum_a.step(3)
    sum_b.step(2)
    sum_a.step(4)
    to_twins.append(to_twin(full_a.at[pl.ds((1 - core) * 128, 128)], twin_a, 3))
    sum_b.step(3)
    flatten(full_a, codes, half_a)

    @pl.loop(0, BLOCKS)
    def _(i):
        cols = pl.ds(pl.multiple_of(i * BLOCK, BLOCK), BLOCK)
        lifted = lax.dot_general(codes[...], u[cols, :], NT, preferred_element_type=F32)
        base[:, cols] = c[:, cols].astype(F32) * (lifted + b_ref[:, cols] + 1.0)

    to_twins[3].wait_recv()
    other_half(twin_a, half_a)
    to_twins[1].wait_recv()

    @pl.loop(0, BLOCKS)
    def _(i):
        rows = pl.ds(pl.multiple_of(i * BLOCK, BLOCK), BLOCK)
        value = jnp.dot(dt[0, rows, :], half_a[0], preferred_element_type=F32)
        value += jnp.dot(dt[1, rows, :], half_a[1], preferred_element_type=F32)
        gu[rows, :] = value.astype(BF16)

    to_twins[0].wait_recv()
    gb_ref[...] = bias_own[0:1, :] + bias_twin[0:1, :]

    sum_b.step(4)
    to_twins.append(to_twin(full_b.at[pl.ds((1 - core) * 128, 128)], twin_b, 4))
    flatten(full_b, dcodes, half_b)

    @pl.loop(0, BLOCKS)
    def _(i):
        cols = pl.ds(pl.multiple_of(i * BLOCK, BLOCK), BLOCK)
        back = lax.dot_general(dcodes[...], v[cols, :], NT, preferred_element_type=F32)
        gi[:, cols] = (base[:, cols] + back).astype(BF16)

    to_twins[4].wait_recv()
    other_half(twin_b, half_b)
    to_twins[2].wait_recv()
    sum_a.finish()
    sum_b.finish()
    for copy in to_twins:
        copy.wait_send()


def last_kernel(gi, gu, ft, half_b, gb, gi_hbm, gu_hbm, gv_hbm, gb_hbm, gv, sem):
    copies = [
        pltpu.make_async_copy(gi, gi_hbm, sem.at[0]),
        pltpu.make_async_copy(gu, gu_hbm, sem.at[1]),
        pltpu.make_async_copy(gb, gb_hbm, sem.at[2]),
    ]
    for copy in copies:
        copy.start()
    for i in range(BLOCKS):
        rows = pl.ds(i * BLOCK, BLOCK)
        value = jnp.dot(ft[0, rows, :], half_b[0], preferred_element_type=F32)
        value += jnp.dot(ft[1, rows, :], half_b[1], preferred_element_type=F32)
        gv[rows, :] = value.astype(BF16)
        copies.append(pltpu.make_async_copy(gv.at[rows, :], gv_hbm.at[rows, :], sem.at[3 + i]))
        copies[-1].start()
    for copy in copies:
        copy.wait()


def shards(features, cotangent, u_rows, v_rows, bias):
    anywhere, vmem = pl.BlockSpec(memory_space=pl.ANY), pl.BlockSpec(memory_space=pltpu.VMEM)
    tiles = (TILES, 16, 128)
    dma = pltpu.SemaphoreType.DMA
    inner = pl.pallas_call(
        kernel,
        out_shape=(
            pltpu.VMEM((ROWS, COLS), BF16),
            pltpu.VMEM((COLS, HALF), BF16),
            pltpu.VMEM((2, COLS, ROWS), BF16),
            pltpu.VMEM((2, ROWS, HALF), BF16),
            pltpu.VMEM((1, COLS), F32),
        ),
        in_specs=[anywhere] * 4 + [vmem],
        out_specs=(vmem,) * 5,
        scratch_shapes=[
            pltpu.VMEM((ROWS, COLS), BF16), pltpu.VMEM((ROWS, COLS), BF16),
            pltpu.VMEM((COLS, RANK), BF16), pltpu.VMEM((COLS, RANK), BF16),
            pltpu.VMEM((ROWS, COLS), BF16),
            pltpu.VMEM(tiles, F32), pltpu.VMEM(tiles, F32),
            pltpu.VMEM(tiles, BF16), pltpu.VMEM(tiles, BF16),
            pltpu.VMEM((288, 16, 128), BF16), pltpu.VMEM((288, 16, 128), BF16),
            pltpu.VMEM((16, 16, 128), BF16), pltpu.VMEM((16, 16, 128), BF16),
            pltpu.VMEM(tiles, BF16), pltpu.VMEM(tiles, BF16),
            pltpu.VMEM((2, COLS, ROWS), BF16),
            pltpu.VMEM((ROWS, COLS), F32),
            pltpu.VMEM((ROWS, RANK), BF16), pltpu.VMEM((ROWS, RANK), BF16),
            pltpu.VMEM((2, ROWS, HALF), BF16),
            pltpu.VMEM((128, 16, 128), BF16), pltpu.VMEM((128, 16, 128), BF16),
            pltpu.VMEM((8, COLS), F32), pltpu.VMEM((8, COLS), F32),
            dma((10,)),
            dma((STAGES, PARTS, 3)), dma((STAGES, PARTS, 3)), dma((STAGES, PARTS, 3)), dma((STAGES, PARTS, 3)),
            dma((5,)), dma((5,)),
        ],
        compiler_params=pltpu.CompilerParams(collective_id=0, has_side_effects=True, vmem_limit_bytes=46 << 20),
    )(features, cotangent, u_rows, v_rows, bias.reshape(1, COLS))
    grad_input, grad_u, grad_v, grad_bias = pl.pallas_call(
        last_kernel,
        out_shape=(
            jax.ShapeDtypeStruct((ROWS, COLS), BF16),
            jax.ShapeDtypeStruct((COLS, HALF), BF16),
            jax.ShapeDtypeStruct((COLS, HALF), BF16),
            jax.ShapeDtypeStruct((1, COLS), F32),
        ),
        in_specs=[vmem] * 5,
        out_specs=(anywhere,) * 4,
        scratch_shapes=[pltpu.VMEM((COLS, HALF), BF16), dma((3 + BLOCKS,))],
        compiler_params=pltpu.CompilerParams(vmem_limit_bytes=16 << 20),
    )(*inner)
    return grad_input, grad_u, grad_v, grad_bias.reshape(COLS)


def solution(mesh):
    in_specs = (P("batch", "feat"), P("batch", "feat"), P("feat", None), P("feat", None), P("feat"))
    out_specs = (P("batch", "feat"), P("feat", "batch"), P("feat", "batch"), P("feat"))
    return jax.shard_map(shards, mesh=mesh, in_specs=in_specs, out_specs=out_specs, check_vma=False)
```

```python
import jax
import jax.numpy as jnp
from jax import lax
from jax.experimental import pallas as pl
from jax.experimental.pallas import tpu as pltpu
from jax.sharding import PartitionSpec as P

MESH = pl.DeviceIdType.MESH
F32, BF16 = jnp.float32, jnp.bfloat16
NT = (((1,), (1,)), ((), ()))
ROWS, COLS, RANK = 512, 2048, 1024
HALF, BLOCK = RANK // 2, 256
BLOCKS = COLS // BLOCK
TILES = 256
STAGES, PARTS = 5, 3
SIZES = ((96, 80, 80), (80, 96, 80))
AXES = ((16, 0), (4, 0), (1, 0), (16, 1), (4, 1), (1, 1))
PAIRS = ((0, 4), (1, 5), (2, 3))


def hypercube(feat):
    bits, steps = [], []
    for stride, kind in AXES:
        place = lax.rem(lax.div(feat, stride), 4)
        if kind == 0:
            bits.append(lax.rem(lax.div(place + 1, 2), 2))
            steps.append((1 - 2 * lax.rem(place, 2)) * stride)
        else:
            bits.append(lax.div(place, 2))
            steps.append((3 - 2 * place) * stride)
    return bits, steps


def squares(feat):
    bits, steps = hypercube(feat)
    result = []
    for high, low in PAIRS:
        quarters, chips = [], []
        for flip in range(4):
            far, near = flip // 2, flip % 2
            quarters.append(2 * (1 - bits[high] if far else bits[high]) + (1 - bits[low] if near else bits[low]))
            chips.append(feat + far * steps[high] + near * steps[low])
        result.append((quarters, chips))
    return result


class Sum:
    def __init__(self, index, places, core, acc, out, got, mid, full, send_sem, recv_sem):
        self.index, self.places, self.core = index, places, core
        self.acc, self.out, self.got, self.mid, self.full = acc, out, got, mid, full
        self.send_sem, self.recv_sem = send_sem, recv_sem
        self.sizes = SIZES[index]
        self.starts = [sum(self.sizes[:part]) for part in range(PARTS)]
        self.copies, self.past = {}, {}
        self.region = dict(enumerate(zip(self.starts, self.sizes)))
        offset, self.offset = 0, {}
        for stage in range(3):
            for part in range(PARTS):
                self.offset[stage, part] = offset
                offset += 3 * (self.sizes[part] >> min(2 * stage + 2, 4))

    def square(self, part, stage):
        return self.places[(part + min(stage, STAGES - 1 - stage) + self.index) % PARTS]

    def slot(self, part, stage, flip, size):
        return pl.ds(self.offset[stage, part] + (flip - 1) * size, size)

    def send(self, part, stage):
        quarters, chips = self.square(part, stage)
        start, size = self.region[part]
        if stage < 2:
            size //= 4
            self.past[stage, part] = start
            self.region[part] = (start + quarters[0] * size, size)
        for flip in (3, 2, 1):
            if stage < 2:
                source = self.out.at[pl.ds(start + quarters[flip] * size, size)]
                target = self.got.at[self.slot(part, stage, flip, size)]
            elif stage == 2:
                source = self.mid.at[pl.ds(self.starts[part] // 16, size)]
                target = self.got.at[self.slot(part, stage, flip, size)]
            else:
                source = target = self.full.at[pl.ds(start, size)]
            copy = pltpu.make_async_remote_copy(
                src_ref=source,
                dst_ref=target,
                send_sem=self.send_sem.at[stage, part, flip - 1],
                recv_sem=self.recv_sem.at[stage, part, flip - 1],
                device_id=(chips[flip], self.core),
                device_id_type=MESH,
            )
            copy.start()
            self.copies[stage, part, flip] = copy

    def receive(self, part, stage):
        for flip in (1, 2, 3):
            self.copies[stage, part, flip].wait_recv()
        start, size = self.region[part]
        if stage > 2:
            self.region[part] = (self.past[STAGES - 1 - stage, part], 4 * size)
            return
        here = pl.ds(start, size)
        value = self.acc[here]
        for flip in (1, 2, 3):
            value += self.got[self.slot(part, stage, flip, size)].astype(F32)
        if stage == 2:
            self.full[here] = value.astype(BF16)
            return
        self.acc[here] = value
        if stage == 0:
            self.out[here] = value.astype(BF16)
        else:
            self.mid[pl.ds(self.starts[part] // 16, size)] = value.astype(BF16)

    def step(self, stage):
        for part in range(PARTS):
            self.receive(part, stage)
            if stage + 1 < STAGES:
                self.send(part, stage + 1)

    def finish(self):
        for copy in self.copies.values():
            copy.wait_send()


def kernel(
    f_hbm, c_hbm, u_hbm, v_hbm, b_ref, gi, gu, ft, half_b, gb_ref,
    f, c, u, v, d, acc_a, acc_b, out_a, out_b, got_a, got_b, mid_a, mid_b, full_a, full_b,
    dt, base, codes, dcodes, half_a, twin_a, twin_b, bias_own, bias_twin,
    load_sem, send_a, recv_a, send_b, recv_b, twin_send, twin_recv,
):
    feat, core = lax.axis_index("feat"), lax.axis_index("batch")
    twin = (feat, 1 - core)
    places = squares(feat)

    loads = {}

    def load(name, source, target):
        loads[name] = pltpu.make_async_copy(source, target, load_sem.at[len(loads)])
        loads[name].start()

    def load_block(name, source, target, j):
        cols = pl.ds(j * BLOCK, BLOCK)
        load((name, j), source.at[:, cols], target.at[:, cols])

    load("f", f_hbm, f)
    load_block("v", v_hbm, v, 0)
    load_block("v", v_hbm, v, 1)
    load("c", c_hbm, c)
    load_block("v", v_hbm, v, 2)
    load_block("v", v_hbm, v, 3)
    for j in range(4):
        load_block("u", u_hbm, u, j)

    barrier = pltpu.get_barrier_semaphore()
    for _, chips in places:
        for flip in (1, 2, 3):
            pl.semaphore_signal(barrier, inc=1, device_id=(chips[flip], core), device_id_type=MESH)
    pl.semaphore_signal(barrier, inc=1, device_id=twin, device_id_type=MESH)

    sum_a = Sum(0, places, core, acc_a, out_a, got_a, mid_a, full_a, send_a, recv_a)
    sum_b = Sum(1, places, core, acc_b, out_b, got_b, mid_b, full_b, send_b, recv_b)

    def partial(left, right, total, j):
        block = jnp.dot(left[...], right[:, j * BLOCK:(j + 1) * BLOCK], preferred_element_type=F32)
        for side in range(2):
            tiles = block[:, side * 128:(side + 1) * 128].reshape(32, 16, 128)
            where = pl.ds(64 * j + 32 * side, 32)
            total.acc[where] = tiles
            total.out[where] = tiles.astype(BF16)

    def first_sends(total, j):
        for part in range(PARTS):
            end = total.starts[part] + total.sizes[part]
            if 64 * j < end <= 64 * (j + 1):
                total.send(part, 0)

    def lift(lower, upper):
        for i in range(lower, upper, BLOCK):
            cols = slice(i, i + BLOCK)
            d[:, cols] = (c[:, cols].astype(F32) * f[:, cols].astype(F32)).astype(BF16)

    loads["f"].wait()
    for j in range(4):
        loads["v", j].wait()
        if j == 2:
            loads["c"].wait()
        partial(f, v, sum_a, j)
        if j >= 2:
            lift((j - 2) * COLS // 2, (j - 1) * COLS // 2)
        if j == 1:
            pl.semaphore_wait(barrier, 10)
        first_sends(sum_a, j)
    for j in range(4):
        loads["u", j].wait()
        partial(d, u, sum_b, j)
        first_sends(sum_b, j)

    def to_twin(source, target, k):
        copy = pltpu.make_async_remote_copy(
            src_ref=source, dst_ref=target, send_sem=twin_send.at[k], recv_sem=twin_recv.at[k],
            device_id=twin, device_id_type=MESH,
        )
        copy.start()
        return copy

    to_twins = {}
    for k, (source, target) in enumerate(((d, dt), (f, ft))):
        for i in range(0, COLS, BLOCK):
            target[core, i:i + BLOCK, :] = source[:, i:i + BLOCK].T
        to_twins[k] = to_twin(target.at[core], target.at[core], k)
    for i in range(0, COLS, BLOCK):
        total = jnp.sum(d[:, i:i + BLOCK].astype(F32), axis=0, keepdims=True)
        bias_own[:, i:i + BLOCK] = jnp.broadcast_to(total, (8, BLOCK))
    to_twins[2] = to_twin(bias_own, bias_twin, 2)

    def flatten(full, flat, half):
        for j in range(8):
            flat[:, j * 128:(j + 1) * 128] = full[32 * j:32 * (j + 1)].reshape(ROWS, 128)
        for j in range(4):
            half[core, :, j * 128:(j + 1) * 128] = full[pl.ds(core * 128 + 32 * j, 32)].reshape(ROWS, 128)

    def other_half(other, half):
        for j in range(4):
            half[1 - core, :, j * 128:(j + 1) * 128] = other[32 * j:32 * (j + 1)].reshape(ROWS, 128)

    for total, stage in (
        (sum_a, 0), (sum_a, 1), (sum_b, 0), (sum_a, 2), (sum_b, 1), (sum_a, 3), (sum_b, 2), (sum_b, 3), (sum_a, 4),
    ):
        total.step(stage)
    to_twins[3] = to_twin(full_a.at[pl.ds((1 - core) * 128, 128)], twin_a, 3)
    flatten(full_a, codes, half_a)
    for i in range(0, COLS, BLOCK):
        cols = slice(i, i + BLOCK)
        lifted = lax.dot_general(codes[...], u[cols, :], NT, preferred_element_type=F32)
        base[:, cols] = c[:, cols].astype(F32) * (lifted + b_ref[:, cols] + 1.0)
    to_twins[3].wait_recv()
    other_half(twin_a, half_a)
    to_twins[0].wait_recv()
    for i in range(0, COLS, BLOCK):
        value = jnp.dot(dt[0, i:i + BLOCK, :], half_a[0], preferred_element_type=F32)
        value += jnp.dot(dt[1, i:i + BLOCK, :], half_a[1], preferred_element_type=F32)
        gu[i:i + BLOCK, :] = value.astype(BF16)
    to_twins[2].wait_recv()
    gb_ref[...] = bias_own[0:1, :] + bias_twin[0:1, :]

    sum_b.step(4)
    to_twins[4] = to_twin(full_b.at[pl.ds((1 - core) * 128, 128)], twin_b, 4)
    flatten(full_b, dcodes, half_b)
    for i in range(0, COLS, BLOCK):
        cols = slice(i, i + BLOCK)
        back = lax.dot_general(dcodes[...], v[cols, :], NT, preferred_element_type=F32)
        gi[:, cols] = (base[:, cols] + back).astype(BF16)
    to_twins[4].wait_recv()
    other_half(twin_b, half_b)
    to_twins[1].wait_recv()
    sum_a.finish()
    sum_b.finish()
    for copy in to_twins.values():
        copy.wait_send()


def last_kernel(gi, gu, ft, half_b, gb, gi_hbm, gu_hbm, gv_hbm, gb_hbm, gv, sem):
    copies = [
        pltpu.make_async_copy(gi, gi_hbm, sem.at[0]),
        pltpu.make_async_copy(gu, gu_hbm, sem.at[1]),
        pltpu.make_async_copy(gb, gb_hbm, sem.at[2]),
    ]
    for copy in copies:
        copy.start()
    for i in range(BLOCKS):
        rows = pl.ds(i * BLOCK, BLOCK)
        value = jnp.dot(ft[0, rows, :], half_b[0], preferred_element_type=F32)
        value += jnp.dot(ft[1, rows, :], half_b[1], preferred_element_type=F32)
        gv[rows, :] = value.astype(BF16)
        copies.append(pltpu.make_async_copy(gv.at[rows, :], gv_hbm.at[rows, :], sem.at[3 + i]))
        copies[-1].start()
    for copy in copies:
        copy.wait()


def shards(features, cotangent, u_rows, v_rows, bias):
    anywhere, vmem = pl.BlockSpec(memory_space=pl.ANY), pl.BlockSpec(memory_space=pltpu.VMEM)
    tiles = (TILES, 16, 128)
    dma = pltpu.SemaphoreType.DMA
    inner = pl.pallas_call(
        kernel,
        out_shape=(
            pltpu.VMEM((ROWS, COLS), BF16),
            pltpu.VMEM((COLS, HALF), BF16),
            pltpu.VMEM((2, COLS, ROWS), BF16),
            pltpu.VMEM((2, ROWS, HALF), BF16),
            pltpu.VMEM((1, COLS), F32),
        ),
        in_specs=[anywhere] * 4 + [vmem],
        out_specs=(vmem,) * 5,
        scratch_shapes=[
            pltpu.VMEM((ROWS, COLS), BF16), pltpu.VMEM((ROWS, COLS), BF16),
            pltpu.VMEM((COLS, RANK), BF16), pltpu.VMEM((COLS, RANK), BF16),
            pltpu.VMEM((ROWS, COLS), BF16),
            pltpu.VMEM(tiles, F32), pltpu.VMEM(tiles, F32),
            pltpu.VMEM(tiles, BF16), pltpu.VMEM(tiles, BF16),
            pltpu.VMEM((288, 16, 128), BF16), pltpu.VMEM((288, 16, 128), BF16),
            pltpu.VMEM((16, 16, 128), BF16), pltpu.VMEM((16, 16, 128), BF16),
            pltpu.VMEM(tiles, BF16), pltpu.VMEM(tiles, BF16),
            pltpu.VMEM((2, COLS, ROWS), BF16),
            pltpu.VMEM((ROWS, COLS), F32),
            pltpu.VMEM((ROWS, RANK), BF16), pltpu.VMEM((ROWS, RANK), BF16),
            pltpu.VMEM((2, ROWS, HALF), BF16),
            pltpu.VMEM((128, 16, 128), BF16), pltpu.VMEM((128, 16, 128), BF16),
            pltpu.VMEM((8, COLS), F32), pltpu.VMEM((8, COLS), F32),
            dma((10,)),
            dma((STAGES, PARTS, 3)), dma((STAGES, PARTS, 3)), dma((STAGES, PARTS, 3)), dma((STAGES, PARTS, 3)),
            dma((5,)), dma((5,)),
        ],
        compiler_params=pltpu.CompilerParams(collective_id=0, has_side_effects=True, vmem_limit_bytes=46 << 20),
    )(features, cotangent, u_rows, v_rows, bias.reshape(1, COLS))
    grad_input, grad_u, grad_v, grad_bias = pl.pallas_call(
        last_kernel,
        out_shape=(
            jax.ShapeDtypeStruct((ROWS, COLS), BF16),
            jax.ShapeDtypeStruct((COLS, HALF), BF16),
            jax.ShapeDtypeStruct((COLS, HALF), BF16),
            jax.ShapeDtypeStruct((1, COLS), F32),
        ),
        in_specs=[vmem] * 5,
        out_specs=(anywhere,) * 4,
        scratch_shapes=[pltpu.VMEM((COLS, HALF), BF16), dma((3 + BLOCKS,))],
        compiler_params=pltpu.CompilerParams(vmem_limit_bytes=16 << 20),
    )(*inner)
    return grad_input, grad_u, grad_v, grad_bias.reshape(COLS)


def solution(mesh):
    in_specs = (P("batch", "feat"), P("batch", "feat"), P("feat", None), P("feat", None), P("feat"))
    out_specs = (P("batch", "feat"), P("feat", "batch"), P("feat", "batch"), P("feat"))
    return jax.shard_map(shards, mesh=mesh, in_specs=in_specs, out_specs=out_specs, check_vma=False)
```

```python
import jax
import jax.numpy as jnp
from jax import lax
from jax.experimental import pallas as pl
from jax.experimental.pallas import tpu as pltpu
from jax.sharding import PartitionSpec as P

MESH = pl.DeviceIdType.MESH
F32, BF16 = jnp.float32, jnp.bfloat16
NT = (((1,), (1,)), ((), ()))
ROWS, COLS, RANK = 512, 2048, 1024
HALF, BLOCK = RANK // 2, 256
BLOCKS = COLS // BLOCK
TILES = 256
STAGES, PARTS = 5, 3
SIZES = ((96, 80, 80), (80, 96, 80))
AXES = ((16, 0), (4, 0), (1, 0), (16, 1), (4, 1), (1, 1))
PAIRS = ((0, 3), (1, 4), (2, 5))


def hypercube(feat):
    bits, steps = [], []
    for stride, kind in AXES:
        place = lax.rem(lax.div(feat, stride), 4)
        if kind == 0:
            bits.append(lax.rem(lax.div(place + 1, 2), 2))
            steps.append((1 - 2 * lax.rem(place, 2)) * stride)
        else:
            bits.append(lax.div(place, 2))
            steps.append((3 - 2 * place) * stride)
    return bits, steps


def squares(feat):
    bits, steps = hypercube(feat)
    result = []
    for high, low in PAIRS:
        quarters, chips = [], []
        for flip in range(4):
            far, near = flip // 2, flip % 2
            quarters.append(2 * (1 - bits[high] if far else bits[high]) + (1 - bits[low] if near else bits[low]))
            if flip == 3:
                stride = AXES[high][0]
                place = lax.rem(lax.div(feat, stride), 4)
                chips.append(feat + (lax.rem(place + 2, 4) - place) * stride)
            else:
                chips.append(feat + far * steps[high] + near * steps[low])
        result.append((quarters, chips))
    return result


class Sum:
    def __init__(self, index, places, core, acc, out, got, mid, full, send_sem, recv_sem):
        self.index, self.places, self.core = index, places, core
        self.acc, self.out, self.got, self.mid, self.full = acc, out, got, mid, full
        self.send_sem, self.recv_sem = send_sem, recv_sem
        self.sizes = SIZES[index]
        self.starts = [sum(self.sizes[:part]) for part in range(PARTS)]
        self.copies, self.past = {}, {}
        self.region = dict(enumerate(zip(self.starts, self.sizes)))
        offset, self.offset = 0, {}
        for stage in range(3):
            for part in range(PARTS):
                self.offset[stage, part] = offset
                offset += 3 * (self.sizes[part] >> min(2 * stage + 2, 4))

    def square(self, part, stage):
        return self.places[(part + min(stage, STAGES - 1 - stage) + self.index) % PARTS]

    def slot(self, part, stage, flip, size):
        return pl.ds(self.offset[stage, part] + (flip - 1) * size, size)

    def send(self, part, stage):
        quarters, chips = self.square(part, stage)
        start, size = self.region[part]
        if stage < 2:
            size //= 4
            self.past[stage, part] = start
            self.region[part] = (start + quarters[0] * size, size)
        for flip in (3, 1, 2):
            if stage < 2:
                source = self.out.at[pl.ds(start + quarters[flip] * size, size)]
                target = self.got.at[self.slot(part, stage, flip, size)]
            elif stage == 2:
                source = self.mid.at[pl.ds(self.starts[part] // 16, size)]
                target = self.got.at[self.slot(part, stage, flip, size)]
            else:
                source = target = self.full.at[pl.ds(start, size)]
            copy = pltpu.make_async_remote_copy(
                src_ref=source,
                dst_ref=target,
                send_sem=self.send_sem.at[stage, part, flip - 1],
                recv_sem=self.recv_sem.at[stage, part, flip - 1],
                device_id=(chips[flip], self.core),
                device_id_type=MESH,
            )
            copy.start()
            self.copies[stage, part, flip] = copy

    def receive(self, part, stage):
        for flip in (1, 2, 3):
            self.copies[stage, part, flip].wait_recv()
        start, size = self.region[part]
        if stage > 2:
            self.region[part] = (self.past[STAGES - 1 - stage, part], 4 * size)
            return
        here = pl.ds(start, size)
        value = self.acc[here]
        for flip in (1, 2, 3):
            value += self.got[self.slot(part, stage, flip, size)].astype(F32)
        if stage == 2:
            self.full[here] = value.astype(BF16)
            return
        self.acc[here] = value
        if stage == 0:
            self.out[here] = value.astype(BF16)
        else:
            self.mid[pl.ds(self.starts[part] // 16, size)] = value.astype(BF16)

    def step(self, stage):
        for part in range(PARTS):
            self.receive(part, stage)
            if stage + 1 < STAGES:
                self.send(part, stage + 1)

    def finish(self, stages):
        for (stage, _, _), copy in self.copies.items():
            if stage in stages:
                copy.wait_send()


def kernel(
    f_hbm, c_hbm, u_hbm, v_hbm, b_ref, gi, gu, ft, half_b, gb_ref,
    f, c, u, v, d, acc_a, acc_b, out_a, out_b, got_a, got_b, mid_a, mid_b, full_a, full_b,
    dt, base, codes, dcodes, half_a, twin_a, twin_b, bias_own, bias_twin,
    load_sem, send_a, recv_a, send_b, recv_b, twin_send, twin_recv,
):
    feat, core = lax.axis_index("feat"), lax.axis_index("batch")
    twin = (feat, 1 - core)
    places = squares(feat)

    loads = {}

    def load(name, source, target):
        loads[name] = pltpu.make_async_copy(source, target, load_sem.at[len(loads)])
        loads[name].start()

    def load_block(name, source, target, j):
        cols = pl.ds(j * BLOCK, BLOCK)
        load((name, j), source.at[:, cols], target.at[:, cols])

    load("f", f_hbm, f)
    load_block("v", v_hbm, v, 0)
    load_block("v", v_hbm, v, 1)

    barrier = pltpu.get_barrier_semaphore()
    for _, chips in places:
        for flip in (1, 2, 3):
            pl.semaphore_signal(barrier, inc=1, device_id=(chips[flip], core), device_id_type=MESH)
    pl.semaphore_signal(barrier, inc=1, device_id=twin, device_id_type=MESH)

    sum_a = Sum(0, places, core, acc_a, out_a, got_a, mid_a, full_a, send_a, recv_a)
    sum_b = Sum(1, places, core, acc_b, out_b, got_b, mid_b, full_b, send_b, recv_b)

    def partial(left, right, total, j):
        block = jnp.dot(left[...], right[:, j * BLOCK:(j + 1) * BLOCK], preferred_element_type=F32)
        for side in range(2):
            tiles = block[:, side * 128:(side + 1) * 128].reshape(32, 16, 128)
            where = pl.ds(64 * j + 32 * side, 32)
            total.acc[where] = tiles
            total.out[where] = tiles.astype(BF16)

    def first_sends(total, j):
        for part in range(PARTS):
            end = total.starts[part] + total.sizes[part]
            if 64 * j < end <= 64 * (j + 1):
                total.send(part, 0)

    loads["f"].wait()
    load_block("v", v_hbm, v, 2)
    load_block("v", v_hbm, v, 3)
    load("c", c_hbm, c)
    for j in range(4):
        loads["v", j].wait()
        if j == 0:
            for k in range(4):
                load_block("u", u_hbm, u, k)
        partial(f, v, sum_a, j)
        if j == 1:
            pl.semaphore_wait(barrier, 10)
        first_sends(sum_a, j)
    loads["c"].wait()
    for i in range(0, COLS, BLOCK):
        d[:, i:i + BLOCK] = c[:, i:i + BLOCK] * f[:, i:i + BLOCK]
    for j in range(4):
        loads["u", j].wait()
        partial(d, u, sum_b, j)
        first_sends(sum_b, j)

    def to_twin(source, target, k):
        copy = pltpu.make_async_remote_copy(
            src_ref=source, dst_ref=target, send_sem=twin_send.at[k], recv_sem=twin_recv.at[k],
            device_id=twin, device_id_type=MESH,
        )
        copy.start()
        return copy

    to_twins = {}
    for k, (source, target) in enumerate(((d, dt), (f, ft))):
        for i in range(0, COLS, BLOCK):
            target[core, i:i + BLOCK, :] = source[:, i:i + BLOCK].T
        to_twins[k] = to_twin(target.at[core], target.at[core], k)
    for i in range(0, COLS, BLOCK):
        total = jnp.sum(d[:, i:i + BLOCK].astype(F32), axis=0, keepdims=True)
        bias_own[:, i:i + BLOCK] = jnp.broadcast_to(total, (8, BLOCK))
    to_twins[2] = to_twin(bias_own, bias_twin, 2)

    def flatten(full, flat, half):
        for j in range(8):
            flat[:, j * 128:(j + 1) * 128] = full[32 * j:32 * (j + 1)].reshape(ROWS, 128)
        for j in range(4):
            half[core, :, j * 128:(j + 1) * 128] = full[pl.ds(core * 128 + 32 * j, 32)].reshape(ROWS, 128)

    def other_half(other, half):
        for j in range(4):
            half[1 - core, :, j * 128:(j + 1) * 128] = other[32 * j:32 * (j + 1)].reshape(ROWS, 128)

    for total, stage in (
        (sum_a, 0), (sum_a, 1), (sum_b, 0), (sum_a, 2), (sum_b, 1), (sum_a, 3), (sum_b, 2), (sum_b, 3), (sum_a, 4),
    ):
        total.step(stage)
    to_twins[3] = to_twin(full_a.at[pl.ds((1 - core) * 128, 128)], twin_a, 3)
    flatten(full_a, codes, half_a)
    for i in range(0, COLS, BLOCK):
        cols = slice(i, i + BLOCK)
        lifted = lax.dot_general(codes[...], u[cols, :], NT, preferred_element_type=F32)
        base[:, cols] = c[:, cols].astype(F32) * (lifted + b_ref[:, cols] + 1.0)
    to_twins[3].wait_recv()
    other_half(twin_a, half_a)
    to_twins[0].wait_recv()
    for i in range(0, COLS, BLOCK):
        value = jnp.dot(dt[0, i:i + BLOCK, :], half_a[0], preferred_element_type=F32)
        value += jnp.dot(dt[1, i:i + BLOCK, :], half_a[1], preferred_element_type=F32)
        gu[i:i + BLOCK, :] = value.astype(BF16)
    to_twins[2].wait_recv()
    gb_ref[...] = bias_own[0:1, :] + bias_twin[0:1, :]

    sum_a.finish(range(STAGES))
    sum_b.finish(range(4))
    for k in range(4):
        to_twins[k].wait_send()
    sum_b.step(4)
    to_twins[4] = to_twin(full_b.at[pl.ds((1 - core) * 128, 128)], twin_b, 4)
    flatten(full_b, dcodes, half_b)
    for i in range(0, COLS, BLOCK):
        cols = slice(i, i + BLOCK)
        back = lax.dot_general(dcodes[...], v[cols, :], NT, preferred_element_type=F32)
        gi[:, cols] = (base[:, cols] + back).astype(BF16)
    to_twins[4].wait_recv()
    other_half(twin_b, half_b)
    to_twins[1].wait_recv()
    sum_b.finish((4,))
    to_twins[4].wait_send()


def last_kernel(gi, gu, ft, half_b, gb, gi_hbm, gu_hbm, gv_hbm, gb_hbm, gv, sem):
    copies = [
        pltpu.make_async_copy(gi, gi_hbm, sem.at[0]),
        pltpu.make_async_copy(gu, gu_hbm, sem.at[1]),
        pltpu.make_async_copy(gb, gb_hbm, sem.at[2]),
    ]
    for copy in copies:
        copy.start()
    for i in range(BLOCKS):
        rows = pl.ds(i * BLOCK, BLOCK)
        value = jnp.dot(ft[0, rows, :], half_b[0], preferred_element_type=F32)
        value += jnp.dot(ft[1, rows, :], half_b[1], preferred_element_type=F32)
        gv[rows, :] = value.astype(BF16)
        copies.append(pltpu.make_async_copy(gv.at[rows, :], gv_hbm.at[rows, :], sem.at[3 + i]))
        copies[-1].start()
    for copy in copies:
        copy.wait()


def shards(features, cotangent, u_rows, v_rows, bias):
    anywhere, vmem = pl.BlockSpec(memory_space=pl.ANY), pl.BlockSpec(memory_space=pltpu.VMEM)
    tiles = (TILES, 16, 128)
    dma = pltpu.SemaphoreType.DMA
    inner = pl.pallas_call(
        kernel,
        out_shape=(
            pltpu.VMEM((ROWS, COLS), BF16),
            pltpu.VMEM((COLS, HALF), BF16),
            pltpu.VMEM((2, COLS, ROWS), BF16),
            pltpu.VMEM((2, ROWS, HALF), BF16),
            pltpu.VMEM((1, COLS), F32),
        ),
        in_specs=[anywhere] * 4 + [vmem],
        out_specs=(vmem,) * 5,
        scratch_shapes=[
            pltpu.VMEM((ROWS, COLS), BF16), pltpu.VMEM((ROWS, COLS), BF16),
            pltpu.VMEM((COLS, RANK), BF16), pltpu.VMEM((COLS, RANK), BF16),
            pltpu.VMEM((ROWS, COLS), BF16),
            pltpu.VMEM(tiles, F32), pltpu.VMEM(tiles, F32),
            pltpu.VMEM(tiles, BF16), pltpu.VMEM(tiles, BF16),
            pltpu.VMEM((288, 16, 128), BF16), pltpu.VMEM((288, 16, 128), BF16),
            pltpu.VMEM((16, 16, 128), BF16), pltpu.VMEM((16, 16, 128), BF16),
            pltpu.VMEM(tiles, BF16), pltpu.VMEM(tiles, BF16),
            pltpu.VMEM((2, COLS, ROWS), BF16),
            pltpu.VMEM((ROWS, COLS), F32),
            pltpu.VMEM((ROWS, RANK), BF16), pltpu.VMEM((ROWS, RANK), BF16),
            pltpu.VMEM((2, ROWS, HALF), BF16),
            pltpu.VMEM((128, 16, 128), BF16), pltpu.VMEM((128, 16, 128), BF16),
            pltpu.VMEM((8, COLS), F32), pltpu.VMEM((8, COLS), F32),
            dma((10,)),
            dma((STAGES, PARTS, 3)), dma((STAGES, PARTS, 3)), dma((STAGES, PARTS, 3)), dma((STAGES, PARTS, 3)),
            dma((5,)), dma((5,)),
        ],
        compiler_params=pltpu.CompilerParams(collective_id=0, has_side_effects=True, vmem_limit_bytes=46 << 20),
    )(features, cotangent, u_rows, v_rows, bias.reshape(1, COLS))
    grad_input, grad_u, grad_v, grad_bias = pl.pallas_call(
        last_kernel,
        out_shape=(
            jax.ShapeDtypeStruct((ROWS, COLS), BF16),
            jax.ShapeDtypeStruct((COLS, HALF), BF16),
            jax.ShapeDtypeStruct((COLS, HALF), BF16),
            jax.ShapeDtypeStruct((1, COLS), F32),
        ),
        in_specs=[vmem] * 5,
        out_specs=(anywhere,) * 4,
        scratch_shapes=[pltpu.VMEM((COLS, HALF), BF16), dma((3 + BLOCKS,))],
        compiler_params=pltpu.CompilerParams(vmem_limit_bytes=16 << 20),
    )(*inner)
    return grad_input, grad_u, grad_v, grad_bias.reshape(COLS)


def solution(mesh):
    in_specs = (P("batch", "feat"), P("batch", "feat"), P("feat", None), P("feat", None), P("feat"))
    out_specs = (P("batch", "feat"), P("feat", "batch"), P("feat", "batch"), P("feat"))
    return jax.shard_map(shards, mesh=mesh, in_specs=in_specs, out_specs=out_specs, check_vma=False)
```

```python
import jax
import jax.numpy as jnp
from jax import lax
from jax.experimental import pallas as pl
from jax.experimental.pallas import tpu as pltpu
from jax.sharding import PartitionSpec as P

MESH = pl.DeviceIdType.MESH
F32, BF16 = jnp.float32, jnp.bfloat16
NT = (((1,), (1,)), ((), ()))
ROWS, COLS, RANK = 512, 2048, 1024
HALF, BLOCK = RANK // 2, 256
BLOCKS = COLS // BLOCK
TILES = 256
STAGES, PARTS = 5, 3
SIZES = ((96, 80, 80), (80, 96, 80))
AXES = ((16, 0), (4, 0), (1, 0), (16, 1), (4, 1), (1, 1))
PAIRS = ((0, 3), (1, 4), (2, 5))


def hypercube(feat):
    bits, steps = [], []
    for stride, kind in AXES:
        place = lax.rem(lax.div(feat, stride), 4)
        if kind == 0:
            bits.append(lax.rem(lax.div(place + 1, 2), 2))
            steps.append((1 - 2 * lax.rem(place, 2)) * stride)
        else:
            bits.append(lax.div(place, 2))
            steps.append((3 - 2 * place) * stride)
    return bits, steps


def squares(feat):
    bits, steps = hypercube(feat)
    result = []
    for high, low in PAIRS:
        quarters, chips = [], []
        for flip in range(4):
            far, near = flip // 2, flip % 2
            quarters.append(2 * (1 - bits[high] if far else bits[high]) + (1 - bits[low] if near else bits[low]))
            if flip == 3:
                stride = AXES[high][0]
                place = lax.rem(lax.div(feat, stride), 4)
                chips.append(feat + (lax.rem(place + 2, 4) - place) * stride)
            else:
                chips.append(feat + far * steps[high] + near * steps[low])
        result.append((quarters, chips))
    return result


class Sum:
    def __init__(self, index, places, core, acc, out, got, mid, full, send_sem, recv_sem):
        self.index, self.places, self.core = index, places, core
        self.acc, self.out, self.got, self.mid, self.full = acc, out, got, mid, full
        self.send_sem, self.recv_sem = send_sem, recv_sem
        self.sizes = SIZES[index]
        self.starts = [sum(self.sizes[:part]) for part in range(PARTS)]
        self.copies, self.past = {}, {}
        self.region = dict(enumerate(zip(self.starts, self.sizes)))
        offset, self.offset = 0, {}
        for stage in range(3):
            for part in range(PARTS):
                self.offset[stage, part] = offset
                offset += 3 * (self.sizes[part] >> min(2 * stage + 2, 4))

    def square(self, part, stage):
        return self.places[(part + min(stage, STAGES - 1 - stage) + self.index) % PARTS]

    def slot(self, part, stage, flip, size):
        return pl.ds(self.offset[stage, part] + (flip - 1) * size, size)

    def send(self, part, stage):
        quarters, chips = self.square(part, stage)
        start, size = self.region[part]
        if stage < 2:
            size //= 4
            self.past[stage, part] = start
            self.region[part] = (start + quarters[0] * size, size)
        for flip in (3, 1, 2):
            if stage < 2:
                source = self.out.at[pl.ds(start + quarters[flip] * size, size)]
                target = self.got.at[self.slot(part, stage, flip, size)]
            elif stage == 2:
                source = self.mid.at[pl.ds(self.starts[part] // 16, size)]
                target = self.got.at[self.slot(part, stage, flip, size)]
            else:
                source = target = self.full.at[pl.ds(start, size)]
            copy = pltpu.make_async_remote_copy(
                src_ref=source,
                dst_ref=target,
                send_sem=self.send_sem.at[stage, part, flip - 1],
                recv_sem=self.recv_sem.at[stage, part, flip - 1],
                device_id=(chips[flip], self.core),
                device_id_type=MESH,
            )
            copy.start()
            self.copies[stage, part, flip] = copy

    def receive(self, part, stage):
        for flip in (1, 2, 3):
            self.copies[stage, part, flip].wait_recv()
        start, size = self.region[part]
        if stage > 2:
            self.region[part] = (self.past[STAGES - 1 - stage, part], 4 * size)
            return
        here = pl.ds(start, size)
        value = self.acc[here]
        for flip in (1, 2, 3):
            value += self.got[self.slot(part, stage, flip, size)].astype(F32)
        if stage == 2:
            self.full[here] = value.astype(BF16)
            return
        self.acc[here] = value
        if stage == 0:
            self.out[here] = value.astype(BF16)
        else:
            self.mid[pl.ds(self.starts[part] // 16, size)] = value.astype(BF16)

    def step(self, stage):
        for part in range(PARTS):
            self.receive(part, stage)
            if stage + 1 < STAGES:
                self.send(part, stage + 1)

    def finish(self, stages):
        for (stage, _, _), copy in self.copies.items():
            if stage in stages:
                copy.wait_send()


def kernel(
    f_hbm, c_hbm, u_hbm, v_hbm, b_hbm, gi, gu, ft, half_b, gb_ref,
    f, c, u, v, b, d, acc_a, acc_b, out_a, out_b, got_a, got_b, mid_a, mid_b, full_a, full_b,
    dt, base, codes, dcodes, half_a, twin_a, twin_b, bias_own, bias_twin,
    load_sem, send_a, recv_a, send_b, recv_b, twin_send, twin_recv,
):
    feat, core = lax.axis_index("feat"), lax.axis_index("batch")
    twin = (feat, 1 - core)
    places = squares(feat)

    loads = {}

    def load(name, source, target):
        loads[name] = pltpu.make_async_copy(source, target, load_sem.at[len(loads)])
        loads[name].start()

    def load_block(name, source, target, j):
        cols = pl.ds(j * BLOCK, BLOCK)
        load((name, j), source.at[:, cols], target.at[:, cols])

    load("f", f_hbm, f)
    load_block("v", v_hbm, v, 0)
    load_block("v", v_hbm, v, 1)

    barrier = pltpu.get_barrier_semaphore()
    for _, chips in places:
        for flip in (1, 2, 3):
            pl.semaphore_signal(barrier, inc=1, device_id=(chips[flip], core), device_id_type=MESH)
    pl.semaphore_signal(barrier, inc=1, device_id=twin, device_id_type=MESH)

    sum_a = Sum(0, places, core, acc_a, out_a, got_a, mid_a, full_a, send_a, recv_a)
    sum_b = Sum(1, places, core, acc_b, out_b, got_b, mid_b, full_b, send_b, recv_b)

    def partial(left, right, total, j):
        block = jnp.dot(left[...], right[:, j * BLOCK:(j + 1) * BLOCK], preferred_element_type=F32)
        for side in range(2):
            tiles = block[:, side * 128:(side + 1) * 128].reshape(32, 16, 128)
            where = pl.ds(64 * j + 32 * side, 32)
            total.acc[where] = tiles
            total.out[where] = tiles.astype(BF16)

    def first_sends(total, j):
        for part in range(PARTS):
            end = total.starts[part] + total.sizes[part]
            if 64 * j < end <= 64 * (j + 1):
                total.send(part, 0)

    loads["f"].wait()
    load_block("v", v_hbm, v, 2)
    load_block("v", v_hbm, v, 3)
    load("c", c_hbm, c)
    for j in range(4):
        loads["v", j].wait()
        if j == 0:
            for k in range(4):
                load_block("u", u_hbm, u, k)
            load("b", b_hbm, b)
        partial(f, v, sum_a, j)
        if j == 1:
            pl.semaphore_wait(barrier, 10)
        first_sends(sum_a, j)
    loads["c"].wait()
    for i in range(0, COLS, BLOCK):
        d[:, i:i + BLOCK] = c[:, i:i + BLOCK] * f[:, i:i + BLOCK]
    for j in range(4):
        loads["u", j].wait()
        partial(d, u, sum_b, j)
        first_sends(sum_b, j)

    def to_twin(source, target, k):
        copy = pltpu.make_async_remote_copy(
            src_ref=source, dst_ref=target, send_sem=twin_send.at[k], recv_sem=twin_recv.at[k],
            device_id=twin, device_id_type=MESH,
        )
        copy.start()
        return copy

    to_twins = {}
    for k, (source, target) in enumerate(((d, dt), (f, ft))):
        for i in range(0, COLS, BLOCK):
            target[core, i:i + BLOCK, :] = source[:, i:i + BLOCK].T
        to_twins[k] = to_twin(target.at[core], target.at[core], k)
    for i in range(0, COLS, BLOCK):
        total = jnp.sum(d[:, i:i + BLOCK].astype(F32), axis=0, keepdims=True)
        bias_own[:, i:i + BLOCK] = jnp.broadcast_to(total, (8, BLOCK))
    to_twins[2] = to_twin(bias_own, bias_twin, 2)

    def flatten(full, flat, half):
        for j in range(8):
            flat[:, j * 128:(j + 1) * 128] = full[32 * j:32 * (j + 1)].reshape(ROWS, 128)
        for j in range(4):
            half[core, :, j * 128:(j + 1) * 128] = full[pl.ds(core * 128 + 32 * j, 32)].reshape(ROWS, 128)

    def other_half(other, half):
        for j in range(4):
            half[1 - core, :, j * 128:(j + 1) * 128] = other[32 * j:32 * (j + 1)].reshape(ROWS, 128)

    for total, stage in (
        (sum_a, 0), (sum_a, 1), (sum_b, 0), (sum_a, 2), (sum_b, 1), (sum_a, 3), (sum_b, 2), (sum_b, 3), (sum_a, 4),
    ):
        total.step(stage)
    to_twins[3] = to_twin(full_a.at[pl.ds((1 - core) * 128, 128)], twin_a, 3)
    flatten(full_a, codes, half_a)
    loads["b"].wait()
    for i in range(0, COLS, BLOCK):
        cols = slice(i, i + BLOCK)
        lifted = lax.dot_general(codes[...], u[cols, :], NT, preferred_element_type=F32)
        base[:, cols] = c[:, cols].astype(F32) * (lifted + b[:, cols] + 1.0)
    to_twins[3].wait_recv()
    other_half(twin_a, half_a)
    to_twins[0].wait_recv()
    for i in range(0, COLS, BLOCK):
        value = jnp.dot(dt[0, i:i + BLOCK, :], half_a[0], preferred_element_type=F32)
        value += jnp.dot(dt[1, i:i + BLOCK, :], half_a[1], preferred_element_type=F32)
        gu[i:i + BLOCK, :] = value.astype(BF16)
    to_twins[2].wait_recv()
    gb_ref[...] = bias_own[0:1, :] + bias_twin[0:1, :]

    sum_a.finish(range(STAGES))
    sum_b.finish(range(4))
    for k in range(4):
        to_twins[k].wait_send()
    sum_b.step(4)
    to_twins[4] = to_twin(full_b.at[pl.ds((1 - core) * 128, 128)], twin_b, 4)
    flatten(full_b, dcodes, half_b)
    for i in range(0, COLS, BLOCK):
        cols = slice(i, i + BLOCK)
        back = lax.dot_general(dcodes[...], v[cols, :], NT, preferred_element_type=F32)
        gi[:, cols] = (base[:, cols] + back).astype(BF16)
    to_twins[4].wait_recv()
    other_half(twin_b, half_b)
    to_twins[1].wait_recv()
    sum_b.finish((4,))
    to_twins[4].wait_send()


def last_kernel(gi, gu, ft, half_b, gb, gi_hbm, gu_hbm, gv_hbm, gb_hbm, gv, sem):
    copies = [
        pltpu.make_async_copy(gi, gi_hbm, sem.at[0]),
        pltpu.make_async_copy(gu, gu_hbm, sem.at[1]),
        pltpu.make_async_copy(gb, gb_hbm, sem.at[2]),
    ]
    for copy in copies:
        copy.start()
    for i in range(BLOCKS):
        rows = pl.ds(i * BLOCK, BLOCK)
        value = jnp.dot(ft[0, rows, :], half_b[0], preferred_element_type=F32)
        value += jnp.dot(ft[1, rows, :], half_b[1], preferred_element_type=F32)
        gv[rows, :] = value.astype(BF16)
        copies.append(pltpu.make_async_copy(gv.at[rows, :], gv_hbm.at[rows, :], sem.at[3 + i]))
        copies[-1].start()
    for copy in copies:
        copy.wait()


def shards(features, cotangent, u_rows, v_rows, bias):
    anywhere, vmem = pl.BlockSpec(memory_space=pl.ANY), pl.BlockSpec(memory_space=pltpu.VMEM)
    tiles = (TILES, 16, 128)
    dma = pltpu.SemaphoreType.DMA
    inner = pl.pallas_call(
        kernel,
        out_shape=(
            pltpu.VMEM((ROWS, COLS), BF16),
            pltpu.VMEM((COLS, HALF), BF16),
            pltpu.VMEM((2, COLS, ROWS), BF16),
            pltpu.VMEM((2, ROWS, HALF), BF16),
            pltpu.VMEM((1, COLS), F32),
        ),
        in_specs=[anywhere] * 5,
        out_specs=(vmem,) * 5,
        scratch_shapes=[
            pltpu.VMEM((ROWS, COLS), BF16), pltpu.VMEM((ROWS, COLS), BF16),
            pltpu.VMEM((COLS, RANK), BF16), pltpu.VMEM((COLS, RANK), BF16), pltpu.VMEM((1, COLS), F32),
            pltpu.VMEM((ROWS, COLS), BF16),
            pltpu.VMEM(tiles, F32), pltpu.VMEM(tiles, F32),
            pltpu.VMEM(tiles, BF16), pltpu.VMEM(tiles, BF16),
            pltpu.VMEM((288, 16, 128), BF16), pltpu.VMEM((288, 16, 128), BF16),
            pltpu.VMEM((16, 16, 128), BF16), pltpu.VMEM((16, 16, 128), BF16),
            pltpu.VMEM(tiles, BF16), pltpu.VMEM(tiles, BF16),
            pltpu.VMEM((2, COLS, ROWS), BF16),
            pltpu.VMEM((ROWS, COLS), F32),
            pltpu.VMEM((ROWS, RANK), BF16), pltpu.VMEM((ROWS, RANK), BF16),
            pltpu.VMEM((2, ROWS, HALF), BF16),
            pltpu.VMEM((128, 16, 128), BF16), pltpu.VMEM((128, 16, 128), BF16),
            pltpu.VMEM((8, COLS), F32), pltpu.VMEM((8, COLS), F32),
            dma((11,)),
            dma((STAGES, PARTS, 3)), dma((STAGES, PARTS, 3)), dma((STAGES, PARTS, 3)), dma((STAGES, PARTS, 3)),
            dma((5,)), dma((5,)),
        ],
        compiler_params=pltpu.CompilerParams(collective_id=0, has_side_effects=True, vmem_limit_bytes=46 << 20),
    )(features, cotangent, u_rows, v_rows, bias.reshape(1, COLS))
    grad_input, grad_u, grad_v, grad_bias = pl.pallas_call(
        last_kernel,
        out_shape=(
            jax.ShapeDtypeStruct((ROWS, COLS), BF16),
            jax.ShapeDtypeStruct((COLS, HALF), BF16),
            jax.ShapeDtypeStruct((COLS, HALF), BF16),
            jax.ShapeDtypeStruct((1, COLS), F32),
        ),
        in_specs=[vmem] * 5,
        out_specs=(anywhere,) * 4,
        scratch_shapes=[pltpu.VMEM((COLS, HALF), BF16), dma((3 + BLOCKS,))],
        compiler_params=pltpu.CompilerParams(vmem_limit_bytes=16 << 20),
    )(*inner)
    return grad_input, grad_u, grad_v, grad_bias.reshape(COLS)


def solution(mesh):
    in_specs = (P("batch", "feat"), P("batch", "feat"), P("feat", None), P("feat", None), P("feat"))
    out_specs = (P("batch", "feat"), P("feat", "batch"), P("feat", "batch"), P("feat"))
    return jax.shard_map(shards, mesh=mesh, in_specs=in_specs, out_specs=out_specs, check_vma=False)
```

```python
import jax
import jax.numpy as jnp
from jax import lax
from jax.experimental import pallas as pl
from jax.experimental.pallas import tpu as pltpu
from jax.sharding import PartitionSpec as P

MESH = pl.DeviceIdType.MESH
F32, BF16 = jnp.float32, jnp.bfloat16
NT = (((1,), (1,)), ((), ()))
ROWS, COLS, RANK = 512, 2048, 1024
HALF, BLOCK = RANK // 2, 256
BLOCKS = COLS // BLOCK
TILES = 256
STAGES, PARTS = 5, 3
SIZES = ((96, 80, 80), (96, 80, 80))
AXES = ((16, 0), (4, 0), (1, 0), (16, 1), (4, 1), (1, 1))
PAIRS = ((0, 3), (1, 4), (2, 5))


def hypercube(feat):
    bits, steps = [], []
    for stride, kind in AXES:
        place = lax.rem(lax.div(feat, stride), 4)
        if kind == 0:
            bits.append(lax.rem(lax.div(place + 1, 2), 2))
            steps.append((1 - 2 * lax.rem(place, 2)) * stride)
        else:
            bits.append(lax.div(place, 2))
            steps.append((3 - 2 * place) * stride)
    return bits, steps


def squares(feat):
    bits, steps = hypercube(feat)
    result = []
    for high, low in PAIRS:
        quarters, chips = [], []
        for flip in range(4):
            far, near = flip // 2, flip % 2
            quarters.append(2 * (1 - bits[high] if far else bits[high]) + (1 - bits[low] if near else bits[low]))
            if flip == 3:
                stride = AXES[high][0]
                place = lax.rem(lax.div(feat, stride), 4)
                chips.append(feat + (lax.rem(place + 2, 4) - place) * stride)
            else:
                chips.append(feat + far * steps[high] + near * steps[low])
        result.append((quarters, chips))
    return result


class Sum:
    def __init__(self, index, places, core, acc, out, got, mid, full, send_sem, recv_sem):
        self.index, self.places, self.core = index, places, core
        self.acc, self.out, self.got, self.mid, self.full = acc, out, got, mid, full
        self.send_sem, self.recv_sem = send_sem, recv_sem
        self.sizes = SIZES[index]
        self.starts = [sum(self.sizes[:part]) for part in range(PARTS)]
        self.copies, self.past = {}, {}
        self.region = dict(enumerate(zip(self.starts, self.sizes)))
        offset, self.offset = 0, {}
        for stage in range(3):
            for part in range(PARTS):
                self.offset[stage, part] = offset
                offset += 3 * (self.sizes[part] >> min(2 * stage + 2, 4))

    def square(self, part, stage):
        return self.places[(part + min(stage, STAGES - 1 - stage) + self.index) % PARTS]

    def slot(self, part, stage, flip, size):
        return pl.ds(self.offset[stage, part] + (flip - 1) * size, size)

    def send(self, part, stage):
        quarters, chips = self.square(part, stage)
        start, size = self.region[part]
        if stage < 2:
            size //= 4
            self.past[stage, part] = start
            self.region[part] = (start + quarters[0] * size, size)
        for flip in (3, 1, 2):
            if stage < 2:
                source = self.out.at[pl.ds(start + quarters[flip] * size, size)]
                target = self.got.at[self.slot(part, stage, flip, size)]
            elif stage == 2:
                source = self.mid.at[pl.ds(self.starts[part] // 16, size)]
                target = self.got.at[self.slot(part, stage, flip, size)]
            else:
                source = target = self.full.at[pl.ds(start, size)]
            copy = pltpu.make_async_remote_copy(
                src_ref=source,
                dst_ref=target,
                send_sem=self.send_sem.at[stage, part, flip - 1],
                recv_sem=self.recv_sem.at[stage, part, flip - 1],
                device_id=(chips[flip], self.core),
                device_id_type=MESH,
            )
            copy.start()
            self.copies[stage, part, flip] = copy

    def receive(self, part, stage):
        for flip in (1, 2, 3):
            self.copies[stage, part, flip].wait_recv()
        start, size = self.region[part]
        if stage > 2:
            self.region[part] = (self.past[STAGES - 1 - stage, part], 4 * size)
            return
        here = pl.ds(start, size)
        value = self.acc[here]
        for flip in (1, 2, 3):
            value += self.got[self.slot(part, stage, flip, size)].astype(F32)
        if stage == 2:
            self.full[here] = value.astype(BF16)
            return
        self.acc[here] = value
        if stage == 0:
            self.out[here] = value.astype(BF16)
        else:
            self.mid[pl.ds(self.starts[part] // 16, size)] = value.astype(BF16)

    def step(self, stage):
        for part in range(PARTS):
            self.receive(part, stage)
            if stage + 1 < STAGES:
                self.send(part, stage + 1)

    def finish(self, stages):
        for (stage, _, _), copy in self.copies.items():
            if stage in stages:
                copy.wait_send()


def kernel(
    f_hbm, c_hbm, u_hbm, v_hbm, b_hbm, gi, gu, ft, half_b, gb_ref,
    f, c, u, v, b, d, acc_a, acc_b, out_a, out_b, got_a, got_b, mid_a, mid_b, full_a, full_b,
    dt, base, codes, dcodes, half_a, twin_a, twin_b, bias_own, bias_twin,
    load_sem, send_a, recv_a, send_b, recv_b, twin_send, twin_recv,
):
    feat, core = lax.axis_index("feat"), lax.axis_index("batch")
    twin = (feat, 1 - core)
    places = squares(feat)

    loads = {}

    def load(name, source, target):
        loads[name] = pltpu.make_async_copy(source, target, load_sem.at[len(loads)])
        loads[name].start()

    def load_block(name, source, target, j):
        cols = pl.ds(j * BLOCK, BLOCK)
        load((name, j), source.at[:, cols], target.at[:, cols])

    load("f", f_hbm, f)
    load_block("v", v_hbm, v, 0)
    load_block("v", v_hbm, v, 1)

    barrier = pltpu.get_barrier_semaphore()
    for _, chips in places:
        for flip in (1, 2, 3):
            pl.semaphore_signal(barrier, inc=1, device_id=(chips[flip], core), device_id_type=MESH)
    pl.semaphore_signal(barrier, inc=1, device_id=twin, device_id_type=MESH)

    sum_a = Sum(0, places, core, acc_a, out_a, got_a, mid_a, full_a, send_a, recv_a)
    sum_b = Sum(1, places, core, acc_b, out_b, got_b, mid_b, full_b, send_b, recv_b)

    def partial(left, right, total, j):
        block = jnp.dot(left[...], right[:, j * BLOCK:(j + 1) * BLOCK], preferred_element_type=F32)
        for side in range(2):
            tiles = block[:, side * 128:(side + 1) * 128].reshape(32, 16, 128)
            where = pl.ds(64 * j + 32 * side, 32)
            total.acc[where] = tiles
            total.out[where] = tiles.astype(BF16)

    def first_sends(total, j):
        for part in range(PARTS):
            end = total.starts[part] + total.sizes[part]
            if 64 * j < end <= 64 * (j + 1):
                total.send(part, 0)

    loads["f"].wait()
    load_block("v", v_hbm, v, 2)
    load_block("v", v_hbm, v, 3)
    load("c", c_hbm, c)
    for j in range(4):
        loads["v", j].wait()
        if j == 0:
            for k in range(4):
                load_block("u", u_hbm, u, k)
            load("b", b_hbm, b)
        partial(f, v, sum_a, j)
        if j == 1:
            pl.semaphore_wait(barrier, 10)
        first_sends(sum_a, j)
    loads["c"].wait()
    for i in range(0, COLS, BLOCK):
        d[:, i:i + BLOCK] = c[:, i:i + BLOCK] * f[:, i:i + BLOCK]
    for j in range(4):
        loads["u", j].wait()
        partial(d, u, sum_b, j)
        first_sends(sum_b, j)

    def to_twin(source, target, k):
        copy = pltpu.make_async_remote_copy(
            src_ref=source, dst_ref=target, send_sem=twin_send.at[k], recv_sem=twin_recv.at[k],
            device_id=twin, device_id_type=MESH,
        )
        copy.start()
        return copy

    to_twins = {}
    for k, (source, target) in enumerate(((d, dt), (f, ft))):
        for i in range(0, COLS, BLOCK):
            target[core, i:i + BLOCK, :] = source[:, i:i + BLOCK].T
        to_twins[k] = to_twin(target.at[core], target.at[core], k)
    for i in range(0, COLS, BLOCK):
        total = jnp.sum(d[:, i:i + BLOCK].astype(F32), axis=0, keepdims=True)
        bias_own[:, i:i + BLOCK] = jnp.broadcast_to(total, (8, BLOCK))
    to_twins[2] = to_twin(bias_own, bias_twin, 2)

    def flatten(full, flat):
        for j in range(8):
            flat[:, j * 128:(j + 1) * 128] = full[32 * j:32 * (j + 1)].reshape(ROWS, 128)

    def own_half(full, half):
        for j in range(4):
            half[core, :, j * 128:(j + 1) * 128] = full[pl.ds(core * 128 + 32 * j, 32)].reshape(ROWS, 128)

    def other_half(other, half):
        for j in range(4):
            half[1 - core, :, j * 128:(j + 1) * 128] = other[32 * j:32 * (j + 1)].reshape(ROWS, 128)

    for total, stage in (
        (sum_a, 0), (sum_a, 1), (sum_b, 0), (sum_a, 2), (sum_b, 1), (sum_a, 3), (sum_b, 2), (sum_b, 3), (sum_a, 4),
    ):
        total.step(stage)
    to_twins[3] = to_twin(full_a.at[pl.ds((1 - core) * 128, 128)], twin_a, 3)
    flatten(full_a, codes)
    loads["b"].wait()
    for i in range(0, COLS, BLOCK):
        cols = slice(i, i + BLOCK)
        lifted = lax.dot_general(codes[...], u[cols, :], NT, preferred_element_type=F32)
        base[:, cols] = c[:, cols].astype(F32) * (lifted + b[:, cols] + 1.0)
    to_twins[3].wait_recv()
    own_half(full_a, half_a)
    other_half(twin_a, half_a)
    to_twins[0].wait_recv()
    for i in range(0, COLS, BLOCK):
        value = jnp.dot(dt[0, i:i + BLOCK, :], half_a[0], preferred_element_type=F32)
        value += jnp.dot(dt[1, i:i + BLOCK, :], half_a[1], preferred_element_type=F32)
        gu[i:i + BLOCK, :] = value.astype(BF16)
    to_twins[2].wait_recv()
    gb_ref[...] = bias_own[0:1, :] + bias_twin[0:1, :]

    sum_a.finish(range(STAGES))
    sum_b.finish(range(4))
    for k in range(4):
        to_twins[k].wait_send()
    sum_b.step(4)
    to_twins[4] = to_twin(full_b.at[pl.ds((1 - core) * 128, 128)], twin_b, 4)
    flatten(full_b, dcodes)
    for i in range(0, COLS, BLOCK):
        cols = slice(i, i + BLOCK)
        back = lax.dot_general(dcodes[...], v[cols, :], NT, preferred_element_type=F32)
        gi[:, cols] = (base[:, cols] + back).astype(BF16)
    own_half(full_b, half_b)
    to_twins[4].wait_recv()
    other_half(twin_b, half_b)
    to_twins[1].wait_recv()
    sum_b.finish((4,))
    to_twins[4].wait_send()


def last_kernel(gi, gu, ft, half_b, gb, gi_hbm, gu_hbm, gv_hbm, gb_hbm, gv, sem):
    copies = [
        pltpu.make_async_copy(gi, gi_hbm, sem.at[0]),
        pltpu.make_async_copy(gu, gu_hbm, sem.at[1]),
        pltpu.make_async_copy(gb, gb_hbm, sem.at[2]),
    ]
    for copy in copies:
        copy.start()
    for i in range(BLOCKS):
        rows = pl.ds(i * BLOCK, BLOCK)
        value = jnp.dot(ft[0, rows, :], half_b[0], preferred_element_type=F32)
        value += jnp.dot(ft[1, rows, :], half_b[1], preferred_element_type=F32)
        gv[rows, :] = value.astype(BF16)
        copies.append(pltpu.make_async_copy(gv.at[rows, :], gv_hbm.at[rows, :], sem.at[3 + i]))
        copies[-1].start()
    for copy in copies:
        copy.wait()


def shards(features, cotangent, u_rows, v_rows, bias):
    anywhere, vmem = pl.BlockSpec(memory_space=pl.ANY), pl.BlockSpec(memory_space=pltpu.VMEM)
    tiles = (TILES, 16, 128)
    dma = pltpu.SemaphoreType.DMA
    inner = pl.pallas_call(
        kernel,
        out_shape=(
            pltpu.VMEM((ROWS, COLS), BF16),
            pltpu.VMEM((COLS, HALF), BF16),
            pltpu.VMEM((2, COLS, ROWS), BF16),
            pltpu.VMEM((2, ROWS, HALF), BF16),
            pltpu.VMEM((1, COLS), F32),
        ),
        in_specs=[anywhere] * 5,
        out_specs=(vmem,) * 5,
        scratch_shapes=[
            pltpu.VMEM((ROWS, COLS), BF16), pltpu.VMEM((ROWS, COLS), BF16),
            pltpu.VMEM((COLS, RANK), BF16), pltpu.VMEM((COLS, RANK), BF16), pltpu.VMEM((1, COLS), F32),
            pltpu.VMEM((ROWS, COLS), BF16),
            pltpu.VMEM(tiles, F32), pltpu.VMEM(tiles, F32),
            pltpu.VMEM(tiles, BF16), pltpu.VMEM(tiles, BF16),
            pltpu.VMEM((288, 16, 128), BF16), pltpu.VMEM((288, 16, 128), BF16),
            pltpu.VMEM((16, 16, 128), BF16), pltpu.VMEM((16, 16, 128), BF16),
            pltpu.VMEM(tiles, BF16), pltpu.VMEM(tiles, BF16),
            pltpu.VMEM((2, COLS, ROWS), BF16),
            pltpu.VMEM((ROWS, COLS), F32),
            pltpu.VMEM((ROWS, RANK), BF16), pltpu.VMEM((ROWS, RANK), BF16),
            pltpu.VMEM((2, ROWS, HALF), BF16),
            pltpu.VMEM((128, 16, 128), BF16), pltpu.VMEM((128, 16, 128), BF16),
            pltpu.VMEM((8, COLS), F32), pltpu.VMEM((8, COLS), F32),
            dma((11,)),
            dma((STAGES, PARTS, 3)), dma((STAGES, PARTS, 3)), dma((STAGES, PARTS, 3)), dma((STAGES, PARTS, 3)),
            dma((5,)), dma((5,)),
        ],
        compiler_params=pltpu.CompilerParams(collective_id=0, has_side_effects=True, vmem_limit_bytes=46 << 20),
    )(features, cotangent, u_rows, v_rows, bias.reshape(1, COLS))
    grad_input, grad_u, grad_v, grad_bias = pl.pallas_call(
        last_kernel,
        out_shape=(
            jax.ShapeDtypeStruct((ROWS, COLS), BF16),
            jax.ShapeDtypeStruct((COLS, HALF), BF16),
            jax.ShapeDtypeStruct((COLS, HALF), BF16),
            jax.ShapeDtypeStruct((1, COLS), F32),
        ),
        in_specs=[vmem] * 5,
        out_specs=(anywhere,) * 4,
        scratch_shapes=[pltpu.VMEM((COLS, HALF), BF16), dma((3 + BLOCKS,))],
        compiler_params=pltpu.CompilerParams(vmem_limit_bytes=16 << 20),
    )(*inner)
    return grad_input, grad_u, grad_v, grad_bias.reshape(COLS)


def solution(mesh):
    in_specs = (P("batch", "feat"), P("batch", "feat"), P("feat", None), P("feat", None), P("feat"))
    out_specs = (P("batch", "feat"), P("feat", "batch"), P("feat", "batch"), P("feat"))
    return jax.shard_map(shards, mesh=mesh, in_specs=in_specs, out_specs=out_specs, check_vma=False)
```
